32 devices in a mesh: param: 8 (over y, x, core), walker: 4 (over z).
Axes of the slice: x: 2, y: 2, z: 4, core: 2. Of those that a mesh axis runs over, the one named last changes fastest.
Arguments:
- derivs: float32 [32, 4980736], P('walker', 'param'), may hold values from -1.7 to 1.7
- gradient: float32 [4980736], P('param'), may hold values from -0.01171875 to 0.01171875
Outputs:
- solution: float32 [4980736], P(('param', 'walker'))
The draws below stay inside these ranges and needn't reach their ends.
All inputs are finite; a program needn't handle non-finite values.
Results may differ from the reference program's by a relative error of at most 0.0003.
Values sent between devices are 32-bit elements; how exact they have to be, the bound alone decides.
No kernel may reach another device: no remote copies, remote signals or barrier semaphores. Data moves between devices by JAX's collectives and lax.ppermute only.
A program may use at most 64 MiB of HBM per device.

```python
import math
import jax
import jax.numpy as jnp
from jax import lax

P_SIZE = 4980736
ITERS = 3
ROWS = 32


def draw_derivs(key, part):
    key_vals, key_cols, key_rows = jax.random.split(key, 3)
    col_scale = jnp.exp(jax.random.uniform(key_cols, (P_SIZE,), jnp.float32, math.log(0.3), math.log(3.0)))
    ramp = 1.0 + 2.0 * jnp.arange(ROWS, dtype=jnp.float32) / (ROWS - 1)
    row_scale = ramp * jnp.exp(jax.random.uniform(key_rows, (ROWS,), jnp.float32, math.log(0.5), math.log(1.5)))
    values = jax.random.truncated_normal(key_vals, -4.0, 4.0, (ROWS, P_SIZE), jnp.float32)
    return (0.03 * row_scale[:, None] * col_scale[None, :] * values).astype(jnp.float32)


def block_levels(own_key, shape, shards, least, top_value):
    gain = 1.0
    for dim, parts in shards:
        heights = jax.random.uniform(jax.random.fold_in(jax.random.fold_in(own_key, 6), dim), (parts,), jnp.float32, least / len(shards), top_value / len(shards))
        gain = gain * jnp.repeat(jnp.exp(heights), shape[dim] // parts).reshape((-1,) + (1,) * (len(shape) - 1 - dim))
    return gain


def bell_draw(rng, dims, deviation, bound, cuts=(), kind=jnp.bfloat16):
    entries = jax.random.normal(rng, dims, jnp.float32) * deviation
    if len(cuts) > 0:
        entries = block_levels(rng, dims, cuts, -0.22, 0.18) * entries
    return jnp.clip(entries, min=-bound, max=bound).astype(kind)


def setup_inputs(seed: int = 0) -> dict:
    arg_keys = jax.random.split(jax.random.key(seed), 3)
    return {
        "derivs": draw_derivs(jax.random.fold_in(arg_keys[2], 71), 0),
        "gradient": bell_draw(arg_keys[1], (P_SIZE,), 0.002, 0.01171875, ((0, 8),), jnp.float32),
    }


DAMPING = 0.001


def operate(derivs, vector):
    row_vals = jnp.dot(derivs, vector, precision=lax.Precision.HIGHEST)
    back_vals = jnp.dot(row_vals, derivs, precision=lax.Precision.HIGHEST)
    return back_vals / ROWS + DAMPING * vector


def reference(derivs, gradient):
    solution = jnp.zeros_like(gradient)
    residual = gradient
    direction = gradient
    norm_now = jnp.sum(residual * residual)
    for step_idx in range(ITERS):
        image = operate(derivs, direction)
        step_len = norm_now / jnp.sum(direction * image)
        solution = solution + step_len * direction
        residual = residual - step_len * image
        norm_next = jnp.sum(residual * residual)
        direction = residual + (norm_next / norm_now) * direction
        norm_now = norm_next
    return solution
```

```python
import functools

import jax
import jax.numpy as jnp
from jax import lax
from jax.experimental import pallas as pl
from jax.experimental.pallas import tpu as pltpu
from jax.sharding import PartitionSpec as P

DAMPING = 0.001
LANES = 128
SUBLANES = 8
BLOCK_ROWS_MAX = 320
GROUP = 8


def block_rows(rows):
    return max(b for b in range(SUBLANES, BLOCK_ROWS_MAX + 1, SUBLANES) if rows % b == 0)


def lane_total(tile):
    return jnp.broadcast_to(jnp.sum(tile, axis=1, keepdims=True), tile.shape)


def all_total(tile):
    return jnp.broadcast_to(jnp.sum(jnp.sum(tile, axis=0, keepdims=True), axis=1, keepdims=True), tile.shape)


def tile_of(derivs_ref, row):
    return derivs_ref[:, pl.ds(pl.multiple_of(row * LANES, LANES), LANES)]


def products(derivs_ref, vec_ref, rows):
    def step(i, accs):
        accs = list(accs)
        base = i * GROUP
        for s in range(GROUP):
            row = base + s
            lane_vals = jnp.broadcast_to(vec_ref[pl.ds(row, 1), :], (SUBLANES, LANES))
            accs[s % 4] = accs[s % 4] + tile_of(derivs_ref, row) * lane_vals
        return tuple(accs)

    zero = jnp.zeros((SUBLANES, LANES), jnp.float32)
    accs = lax.fori_loop(0, rows // GROUP, step, (zero,) * 4)
    return (accs[0] + accs[1]) + (accs[2] + accs[3])


def tile_sum(block):
    return jnp.sum(block.reshape(-1, SUBLANES, LANES), axis=0)


def start_kernel(steps, derivs_ref, grad_ref, stats_ref):
    step = pl.program_id(0)

    @pl.when(step == 0)
    def _():
        stats_ref[...] = jnp.zeros_like(stats_ref)

    stats_ref[0:8, :] += products(derivs_ref, grad_ref, grad_ref.shape[0])
    grad = grad_ref[...]
    stats_ref[8:16, :] += tile_sum(grad * grad)

    @pl.when(step == steps - 1)
    def _():
        stats_ref[0:8, :] = lane_total(stats_ref[0:8, :])
        stats_ref[8:16, :] = all_total(stats_ref[8:16, :])


def start_call(derivs, grad):
    rows = grad.shape[0]
    blk = block_rows(rows)
    steps = rows // blk
    return pl.pallas_call(
        functools.partial(start_kernel, steps),
        grid=(steps,),
        in_specs=[
            pl.BlockSpec((SUBLANES, blk * LANES), lambda i: (0, i)),
            pl.BlockSpec((blk, LANES), lambda i: (i, 0)),
        ],
        out_specs=pl.BlockSpec((24, LANES), lambda i: (0, 0)),
        out_shape=jax.ShapeDtypeStruct((24, LANES), jnp.float32),
        name="start_products",
    )(derivs, grad)


def back_kernel(derivs_ref, vals_ref, out_ref):
    vals = vals_ref[...]

    def step(i, carry):
        base = i * GROUP
        for s in range(GROUP):
            row = base + s
            out_ref[pl.ds(row, 1), :] = jnp.sum(tile_of(derivs_ref, row) * vals, axis=0, keepdims=True)
        return carry

    lax.fori_loop(0, out_ref.shape[0] // GROUP, step, 0)


def back_call(derivs, vals, rows):
    blk = block_rows(rows)
    return pl.pallas_call(
        back_kernel,
        grid=(rows // blk,),
        in_specs=[
            pl.BlockSpec((SUBLANES, blk * LANES), lambda i: (0, i)),
            pl.BlockSpec((SUBLANES, LANES), lambda i: (0, 0)),
        ],
        out_specs=pl.BlockSpec((blk, LANES), lambda i: (i, 0)),
        out_shape=jax.ShapeDtypeStruct((rows, LANES), jnp.float32),
        name="back_products",
    )(derivs, vals)


def advance_kernel(steps, scale, derivs_ref, res_ref, back_ref, dir_ref, step_ref, new_ref, stats_ref):
    step = pl.program_id(0)

    @pl.when(step == 0)
    def _():
        stats_ref[...] = jnp.zeros_like(stats_ref)

    step_len = step_ref[0:1, :]
    beta = step_ref[1:2, :]
    direction = res_ref[...] + beta * dir_ref[...]
    new = res_ref[...] - step_len * (back_ref[...] * scale + DAMPING * direction)
    new_ref[...] = new
    stats_ref[8:16, :] += tile_sum(new * new)
    stats_ref[16:24, :] += tile_sum(new * direction)
    stats_ref[0:8, :] += products(derivs_ref, new_ref, new_ref.shape[0])

    @pl.when(step == steps - 1)
    def _():
        stats_ref[0:8, :] = lane_total(stats_ref[0:8, :])
        stats_ref[8:16, :] = all_total(stats_ref[8:16, :])
        stats_ref[16:24, :] = all_total(stats_ref[16:24, :])


def advance_call(derivs, residual, back, prev_direction, step_len, beta, rows_all):
    rows = residual.shape[0]
    blk = block_rows(rows)
    steps = rows // blk
    scalars = jnp.concatenate([step_len, beta, jnp.zeros((6, LANES), jnp.float32)])
    vec = pl.BlockSpec((blk, LANES), lambda i: (i, 0))
    return pl.pallas_call(
        functools.partial(advance_kernel, steps, 1.0 / rows_all),
        grid=(steps,),
        in_specs=[
            pl.BlockSpec((SUBLANES, blk * LANES), lambda i: (0, i)),
            vec,
            vec,
            vec,
            pl.BlockSpec((SUBLANES, LANES), lambda i: (0, 0)),
        ],
        out_specs=[vec, pl.BlockSpec((24, LANES), lambda i: (0, 0))],
        out_shape=[
            jax.ShapeDtypeStruct((rows, LANES), jnp.float32),
            jax.ShapeDtypeStruct((24, LANES), jnp.float32),
        ],
        name="advance_residual",
    )(derivs, residual, back, prev_direction, scalars)


def last_kernel(share_ref, grad_ref, res1_ref, res2_ref, coef_ref, out_ref):
    c0, c1, c2 = coef_ref[0:1, :], coef_ref[1:2, :], coef_ref[2:3, :]
    out_ref[...] = c0 * grad_ref[...] + c1 * res1_ref[...] + c2 * res2_ref[...]


def last_call(share, grad, res1, res2, coefs, share_rows):
    vec = pl.BlockSpec((share_rows, LANES), lambda i, share_ref: (share_ref[0], 0))
    return pl.pallas_call(
        last_kernel,
        grid_spec=pltpu.PrefetchScalarGridSpec(
            num_scalar_prefetch=1,
            grid=(1,),
            in_specs=[vec, vec, vec, pl.BlockSpec((SUBLANES, LANES), lambda i, share_ref: (0, 0))],
            out_specs=pl.BlockSpec((share_rows, LANES), lambda i, share_ref: (0, 0)),
        ),
        out_shape=jax.ShapeDtypeStruct((share_rows, LANES), jnp.float32),
        name="last_combination",
    )(share, grad, res1, res2, coefs)


def small_sum(value, axis):
    size = lax.axis_size(axis)
    if size & (size - 1):
        return lax.psum(value, axis)
    bit = 1
    while bit < size:
        value = value + lax.ppermute(value, axis, [(i, i ^ bit) for i in range(size)])
        bit *= 2
    return value


def big_sum(value):
    return lax.psum(value, "walker")


def body(derivs, gradient):
    walkers = lax.axis_size("walker")
    rows_all = derivs.shape[0] * walkers
    rows = gradient.shape[0] // LANES
    grad = gradient.reshape(rows, LANES)

    def walker_squares(vals):
        return small_sum(jnp.sum(vals * vals, axis=0, keepdims=True), "walker")

    stats = small_sum(start_call(derivs, grad), "param")
    vals0, norm0 = stats[0:8], stats[8:9]
    back0 = big_sum(back_call(derivs, vals0, rows))
    dir_sq0 = norm0
    step0 = norm0 / (walker_squares(vals0) / rows_all + DAMPING * dir_sq0)
    zero = jnp.zeros_like(norm0)
    res1, stats = advance_call(derivs, grad, back0, grad, step0, zero, rows_all)

    stats = small_sum(stats, "param")
    norm1, cross1 = stats[8:9], stats[16:17]
    beta1 = norm1 / norm0
    vals1 = stats[0:8] + beta1 * vals0
    back1 = big_sum(back_call(derivs, vals1, rows))
    dir_sq1 = norm1 + 2.0 * beta1 * cross1 + beta1 * beta1 * dir_sq0
    step1 = norm1 / (walker_squares(vals1) / rows_all + DAMPING * dir_sq1)
    res2, stats = advance_call(derivs, res1, back1, grad, step1, beta1, rows_all)

    stats = small_sum(stats, "param")
    norm2, cross2 = stats[8:9], stats[16:17]
    beta2 = norm2 / norm1
    vals2 = stats[0:8] + beta2 * vals1
    dir_sq2 = norm2 + 2.0 * beta2 * cross2 + beta2 * beta2 * dir_sq1
    step2 = norm2 / (walker_squares(vals2) / rows_all + DAMPING * dir_sq2)

    along1 = step1 + step2 * beta2
    coefs = jnp.concatenate([step0 + along1 * beta1, along1, step2, jnp.zeros((5, LANES), jnp.float32)])
    share = lax.axis_index("walker").astype(jnp.int32).reshape(1)
    out = last_call(share, grad, res1, res2, coefs, rows // walkers)
    return out.reshape(-1)


def solution(mesh):
    in_specs = (P("walker", "param"), P("param"))
    out_specs = P(("param", "walker"))
    return jax.shard_map(body, mesh=mesh, in_specs=in_specs, out_specs=out_specs, check_vma=False)
```

```python
import functools

import jax
import jax.numpy as jnp
from jax import lax
from jax.experimental import pallas as pl
from jax.experimental.pallas import tpu as pltpu
from jax.sharding import PartitionSpec as P

DAMPING = 0.001
LANES = 128
SUBLANES = 8
CHUNKS = 8
COPIES = 8
CHUNK_VMEM = 8 * 2**20
EXTRA = 8


def whole_tiles(rows, parts):
    return max(n for n in range(1, parts + 1) if rows % (n * SUBLANES) == 0)


def unroll_of(groups):
    return max(u for u in (1, 2, 4) if groups % u == 0)


def lane_total(tile):
    return jnp.broadcast_to(jnp.sum(tile, axis=1, keepdims=True), tile.shape)


def all_total(tile):
    return lane_total(jnp.broadcast_to(jnp.sum(tile, axis=0, keepdims=True), tile.shape))


def tile_sum(block):
    return jnp.sum(block.reshape(-1, SUBLANES, LANES), axis=0)


def eight_tiles(derivs, row):
    width = SUBLANES * LANES
    block = derivs[:, pl.ds(pl.multiple_of(row * LANES, width), width)]
    return [block[:, s * LANES : (s + 1) * LANES] for s in range(SUBLANES)]


def products(derivs, vec, first, rows, offset=0):
    unroll = unroll_of(rows // SUBLANES)

    def step(i, accs):
        accs = list(accs)
        for u in range(unroll):
            row = first + (i * unroll + u) * SUBLANES
            vals = vec[pl.ds(pl.multiple_of(row, SUBLANES), SUBLANES), :]
            tiles = eight_tiles(derivs, offset + row)
            for s in range(SUBLANES):
                accs[s] = accs[s] + tiles[s] * jnp.broadcast_to(vals[s : s + 1, :], (SUBLANES, LANES))
        return tuple(accs)

    zero = jnp.zeros((SUBLANES, LANES), jnp.float32)
    a = lax.fori_loop(0, rows // SUBLANES // unroll, step, (zero,) * SUBLANES)
    return ((a[0] + a[1]) + (a[2] + a[3])) + ((a[4] + a[5]) + (a[6] + a[7]))


def sublane_sums(tiles):
    index = lax.broadcasted_iota(jnp.int32, (SUBLANES, LANES), 0)
    half = SUBLANES // 2
    while half >= 1:
        low = (index & half) == 0
        merged = []
        for s in range(half):
            a, b = tiles[s], tiles[s + half]
            keep, move = jnp.where(low, a, b), jnp.where(low, b, a)
            if half == SUBLANES // 2:
                moved = pltpu.roll(move, half, 0)
            else:
                moved = jnp.where(low, pltpu.roll(move, SUBLANES - half, 0), pltpu.roll(move, half, 0))
            merged.append(keep + moved)
        tiles = merged
        half //= 2
    return tiles[0]


def vmem():
    return pl.BlockSpec(memory_space=pltpu.VMEM)


def hbm():
    return pl.BlockSpec(memory_space=pltpu.HBM)


def start_kernel(copies, derivs_hbm, grad_hbm, stats, derivs, sems, grad, grad_sems):
    rows = grad.shape[0] // copies
    waits = []
    grad_copies = []
    for c in range(copies):
        part = pl.ds(c * rows, rows)
        grad_copies.append(pltpu.make_async_copy(grad_hbm.at[part, :], grad.at[part, :], grad_sems.at[c]))
        grad_copies[-1].start()
        cols = pl.ds(c * rows * LANES, rows * LANES)
        waits.append(pltpu.make_async_copy(derivs_hbm.at[:, cols], derivs.at[:, cols], sems.at[c]))
        waits[-1].start()
    total = jnp.zeros((SUBLANES, LANES), jnp.float32)
    squares = total
    for c in range(copies):
        grad_copies[c].wait()
        waits[c].wait()
        total = total + products(derivs, grad, c * rows, rows)
        part = grad[c * rows : (c + 1) * rows, :]
        squares = squares + tile_sum(part * part)
    stats[0:8, :] = lane_total(total)
    stats[8:16, :] = all_total(squares)
    stats[16:24, :] = jnp.zeros((SUBLANES, LANES), jnp.float32)


def start_call(derivs, grad):
    rows = grad.shape[0]
    copies = whole_tiles(rows, COPIES)
    return pl.pallas_call(
        functools.partial(start_kernel, copies),
        in_specs=[hbm(), hbm()],
        out_specs=[vmem(), vmem()],
        out_shape=[jax.ShapeDtypeStruct((24, LANES), jnp.float32), pltpu.VMEM(derivs.shape, jnp.float32)],
        scratch_shapes=[
            pltpu.SemaphoreType.DMA((copies,)),
            pltpu.VMEM((rows, LANES), jnp.float32),
            pltpu.SemaphoreType.DMA((copies,)),
        ],
        compiler_params=pltpu.CompilerParams(vmem_limit_bytes=CHUNK_VMEM),
        cost_estimate=pl.CostEstimate(flops=16 * rows * LANES, bytes_accessed=36 * rows * LANES, transcendentals=0),
        name="start_products",
    )(pltpu.with_memory_space_constraint(derivs, pltpu.HBM), pltpu.with_memory_space_constraint(grad, pltpu.HBM))


def back_kernel(offset, derivs, vals_ref, out):
    vals = vals_ref[...]
    rows = out.shape[0] - EXTRA
    out[rows : rows + EXTRA, :] = jnp.broadcast_to(jnp.sum(vals * vals, axis=0, keepdims=True), (EXTRA, LANES))
    unroll = unroll_of(rows // SUBLANES)

    def step(i, carry):
        for u in range(unroll):
            row = (i * unroll + u) * SUBLANES
            tiles = [tile * vals for tile in eight_tiles(derivs, offset + row)]
            out[pl.ds(pl.multiple_of(row, SUBLANES), SUBLANES), :] = sublane_sums(tiles)
        return carry

    lax.fori_loop(0, rows // SUBLANES // unroll, step, 0)


def back_call(derivs, vals, chunk, rows):
    return pl.pallas_call(
        functools.partial(back_kernel, chunk * rows),
        in_specs=[vmem(), vmem()],
        out_specs=vmem(),
        out_shape=jax.ShapeDtypeStruct((rows + EXTRA, LANES), jnp.float32),
        compiler_params=pltpu.CompilerParams(vmem_limit_bytes=CHUNK_VMEM),
        cost_estimate=pl.CostEstimate(flops=16 * rows * LANES, bytes_accessed=36 * rows * LANES, transcendentals=0),
        name="back_products",
    )(pltpu.with_memory_space_constraint(derivs, pltpu.VMEM), vals)


def step_length(norm, squares, rows_all, dir_sq):
    return norm / (squares / rows_all + DAMPING * dir_sq)


def advance_kernel(offset, rows_all, last, derivs, back, squares, known, res, prev, stats_in, new, stats):
    rows = new.shape[0]
    norm, dir_sq, beta = known[0:1, :], known[1:2, :], known[2:3, :]
    step_len = step_length(norm, squares[0:1, :], rows_all, dir_sq)
    old = res[...]
    direction = old + beta * prev[...]
    fresh = old - step_len * (back[0:rows, :] * (1.0 / rows_all) + DAMPING * direction)
    new[...] = fresh
    norms = stats_in[8:16, :] + tile_sum(fresh * fresh)
    cross = stats_in[16:24, :] + tile_sum(fresh * direction)
    total = stats_in[0:8, :] + products(derivs, new, 0, rows, offset)
    if last:
        total, norms, cross = lane_total(total), all_total(norms), all_total(cross)
    stats[0:8, :] = total
    stats[8:16, :] = norms
    stats[16:24, :] = cross


def advance_call(derivs, back, first_back, known, residual, prev, stats, chunk, rows, rows_all, last):
    here = pl.BlockSpec((rows, LANES), lambda i: (0, 0))
    part = pl.BlockSpec((rows, LANES), lambda i: (chunk, 0))
    rest = pl.BlockSpec((EXTRA, LANES), lambda i: (rows // EXTRA, 0))
    tile = pl.BlockSpec((SUBLANES, LANES), lambda i: (0, 0))
    sums = pl.BlockSpec((24, LANES), lambda i: (0, 0))
    return pl.pallas_call(
        functools.partial(advance_kernel, chunk * rows, rows_all, last),
        grid=(1,),
        in_specs=[vmem(), here, rest, tile, here if residual.shape[0] == rows else part, part, sums],
        out_specs=[here, sums],
        out_shape=[
            jax.ShapeDtypeStruct((rows, LANES), jnp.float32),
            jax.ShapeDtypeStruct((24, LANES), jnp.float32),
        ],
        compiler_params=pltpu.CompilerParams(vmem_limit_bytes=CHUNK_VMEM),
        cost_estimate=pl.CostEstimate(flops=24 * rows * LANES, bytes_accessed=48 * rows * LANES, transcendentals=0),
        name="advance_residual",
    )(pltpu.with_memory_space_constraint(derivs, pltpu.VMEM), back, first_back, known, residual, prev, stats)


def last_kernel(share_ref, grad_ref, res1_ref, res2_ref, coef_ref, out_ref):
    c0, c1, c2 = coef_ref[0:1, :], coef_ref[1:2, :], coef_ref[2:3, :]
    out_ref[...] = c0 * grad_ref[...] + c1 * res1_ref[...] + c2 * res2_ref[...]


def last_call(share, grad, res1, res2, coefs, share_rows):
    vec = pl.BlockSpec((share_rows, LANES), lambda i, share_ref: (share_ref[0], 0))
    return pl.pallas_call(
        last_kernel,
        grid_spec=pltpu.PrefetchScalarGridSpec(
            num_scalar_prefetch=1,
            grid=(1,),
            in_specs=[vec, vec, vec, pl.BlockSpec((SUBLANES, LANES), lambda i, share_ref: (0, 0))],
            out_specs=pl.BlockSpec((share_rows, LANES), lambda i, share_ref: (0, 0)),
        ),
        out_shape=jax.ShapeDtypeStruct((share_rows, LANES), jnp.float32),
        name="last_combination",
    )(share, grad, res1, res2, coefs)


def small_sum(value, axis):
    size = lax.axis_size(axis)
    if size & (size - 1):
        return lax.psum(value, axis)
    bit = 1
    while bit < size:
        value = value + lax.ppermute(value, axis, [(i, i ^ bit) for i in range(size)])
        bit *= 2
    return value


def chain(chunks, produce, consume, state, gate):
    count = lax.axis_size("walker")
    me = lax.axis_index("walker")
    gaps = (1, 2)
    up, down = [0], [0]
    for link in range(count - 2):
        up.append(up[-1] + gaps[link % 2])
    for link in range(count - 2, 0, -1):
        down.insert(0, down[0] + gaps[link % 2])

    def links(parity):
        partner, send, recv = {}, {}, {}
        for w in range(count):
            other = w + 1 if w % 2 == parity else w - 1
            if 0 <= other < count:
                link = min(w, other)
                partner[w] = other
                send[w], recv[w] = (up[link], down[link]) if other > w else (down[link], up[link])
        return partner, send, recv

    def pick(items, at, delays):
        found = None
        for delay in sorted(set(delays.values())):
            if not 0 <= at - delay < len(items) or items[at - delay] is None:
                continue
            if found is None:
                found = items[at - delay]
            else:
                mine = functools.reduce(jnp.logical_or, [me == w for w in delays if delays[w] == delay])
                found = jnp.where(mine, items[at - delay], found)
        return found

    both = (links(0), links(1))
    made = [produce(0, gate)]
    got = ([], [])

    def complete(chunk):
        total = made[chunk]
        for parity, (_, _, recv) in enumerate(both):
            arrived = pick(got[parity], chunk, {w: -delay for w, delay in recv.items()})
            if arrived is not None:
                total = total + arrived
        return total

    def exchange(parity, step, before, gate, state):
        partner, send, _ = both[parity]
        pairs = [(w, partner[w]) for w in partner if 0 <= step - send[w] < chunks]
        own = pick(made, step, send) if pairs else None
        if own is None:
            got[parity].append(None)
            return gate, state
        if 0 <= before < step and got[1 - parity][before] is not None:
            own = own + got[1 - parity][before]
        own, gate, *state = lax.optimization_barrier((own, gate, *state))
        got[parity].append(lax.ppermute(own, "walker", pairs))
        return gate, tuple(state)

    late = [max(recv.values(), default=-1) for _, _, recv in both]
    lag = 1 + max(late[0], late[1] + 1)
    steps = chunks + max(late)
    for step in range(steps):
        gate, state = exchange(0, step, step - gaps[1], gate, state)
        if step + 1 < chunks:
            made.append(produce(step + 1, gate))
            made[-1], gate, *state = lax.optimization_barrier((made[-1], gate, *state))
            state = tuple(state)
        gate, state = exchange(1, step, step - gaps[0], gate, state)
        if step - lag >= 0:
            state = consume(step - lag, complete(step - lag), state)
    for chunk in range(max(steps - lag, 0), chunks):
        state = consume(chunk, complete(chunk), state)
    return state


def body(derivs, gradient):
    walkers = lax.axis_size("walker")
    rows_all = derivs.shape[0] * walkers
    rows = gradient.shape[0] // LANES
    grad = gradient.reshape(rows, LANES)
    chunks = whole_tiles(rows, CHUNKS)
    part = rows // chunks

    def advance(residual, prev, vals, norm, dir_sq, beta):
        known = jnp.concatenate([norm, dir_sq, beta, jnp.zeros((5, LANES), jnp.float32)])
        first = []
        fresh = []

        def consume(chunk, total, state):
            if not first:
                first.append(total)
            last = chunk == chunks - 1
            old = residual[chunk] if isinstance(residual, list) else residual
            new, stats = advance_call(
                derivs, total, first[0], known, old, prev, state[0], chunk, part, rows_all, last
            )
            fresh.append(new)
            return (stats,)

        def produce(chunk, gate):
            return back_call(derivs, gate, chunk, part)

        state = (jnp.zeros((24, LANES), jnp.float32),)
        (stats,) = chain(chunks, produce, consume, state, vals)
        step = step_length(norm, first[0][part : part + 1], rows_all, dir_sq)
        return fresh, step, small_sum(stats, "param")

    stats, derivs = start_call(derivs, grad)
    stats = small_sum(stats, "param")
    vals0, norm0 = stats[0:8], stats[8:9]
    dir_sq0 = norm0
    res1, step0, stats = advance(grad, grad, vals0, norm0, dir_sq0, jnp.zeros_like(norm0))

    norm1, cross1 = stats[8:9], stats[16:17]
    beta1 = norm1 / norm0
    vals1 = stats[0:8] + beta1 * vals0
    dir_sq1 = norm1 + 2.0 * beta1 * cross1 + beta1 * beta1 * dir_sq0
    res2, step1, stats = advance(res1, grad, vals1, norm1, dir_sq1, beta1)

    norm2, cross2 = stats[8:9], stats[16:17]
    beta2 = norm2 / norm1
    vals2 = stats[0:8] + beta2 * vals1
    dir_sq2 = norm2 + 2.0 * beta2 * cross2 + beta2 * beta2 * dir_sq1
    squares = small_sum(jnp.sum(vals2 * vals2, axis=0, keepdims=True), "walker")
    step2 = step_length(norm2, squares, rows_all, dir_sq2)

    along1 = step1 + step2 * beta2
    coefs = jnp.concatenate([step0 + along1 * beta1, along1, step2, jnp.zeros((5, LANES), jnp.float32)])
    share = lax.axis_index("walker").astype(jnp.int32).reshape(1)
    out = last_call(share, grad, jnp.concatenate(res1), jnp.concatenate(res2), coefs, rows // walkers)
    return out.reshape(-1)


def solution(mesh):
    in_specs = (P("walker", "param"), P("param"))
    out_specs = P(("param", "walker"))
    return jax.shard_map(body, mesh=mesh, in_specs=in_specs, out_specs=out_specs, check_vma=False)
```

```python
import functools

import jax
import jax.numpy as jnp
from jax import lax
from jax.experimental import pallas as pl
from jax.experimental.pallas import tpu as pltpu
from jax.sharding import PartitionSpec as P

DAMPING = 0.001
LANES = 128
SUBLANES = 8
CHUNKS = 8
COPIES = 8
START_VMEM = 3 * 2**20
BACK_VMEM = 1 * 2**20
ADVANCE_VMEM = 3 * 2**20
EXTRA = 8


def whole_tiles(rows, parts):
    return max(n for n in range(1, parts + 1) if rows % (n * SUBLANES) == 0)


def unroll_of(groups):
    return max(u for u in (1, 2, 4) if groups % u == 0)


def lane_total(tile):
    return jnp.broadcast_to(jnp.sum(tile, axis=1, keepdims=True), tile.shape)


def all_total(tile):
    return lane_total(jnp.broadcast_to(jnp.sum(tile, axis=0, keepdims=True), tile.shape))


def tile_sum(block):
    return jnp.sum(block.reshape(-1, SUBLANES, LANES), axis=0)


def eight_tiles(derivs, row):
    width = SUBLANES * LANES
    block = derivs[:, pl.ds(pl.multiple_of(row * LANES, width), width)]
    return [block[:, s * LANES : (s + 1) * LANES] for s in range(SUBLANES)]


def products(derivs, vec, first, rows, offset=0):
    unroll = unroll_of(rows // SUBLANES)

    def step(i, accs):
        accs = list(accs)
        for u in range(unroll):
            row = first + (i * unroll + u) * SUBLANES
            vals = vec[pl.ds(pl.multiple_of(row, SUBLANES), SUBLANES), :]
            tiles = eight_tiles(derivs, offset + row)
            for s in range(SUBLANES):
                accs[s] = accs[s] + tiles[s] * jnp.broadcast_to(vals[s : s + 1, :], (SUBLANES, LANES))
        return tuple(accs)

    zero = jnp.zeros((SUBLANES, LANES), jnp.float32)
    a = lax.fori_loop(0, rows // SUBLANES // unroll, step, (zero,) * SUBLANES)
    return ((a[0] + a[1]) + (a[2] + a[3])) + ((a[4] + a[5]) + (a[6] + a[7]))


def sublane_sums(tiles):
    index = lax.broadcasted_iota(jnp.int32, (SUBLANES, LANES), 0)
    half = SUBLANES // 2
    while half >= 1:
        low = (index & half) == 0
        merged = []
        for s in range(half):
            a, b = tiles[s], tiles[s + half]
            keep, move = jnp.where(low, a, b), jnp.where(low, b, a)
            if half == SUBLANES // 2:
                moved = pltpu.roll(move, half, 0)
            else:
                moved = jnp.where(low, pltpu.roll(move, SUBLANES - half, 0), pltpu.roll(move, half, 0))
            merged.append(keep + moved)
        tiles = merged
        half //= 2
    return tiles[0]


def vmem():
    return pl.BlockSpec(memory_space=pltpu.VMEM)


def hbm():
    return pl.BlockSpec(memory_space=pltpu.HBM)


def start_kernel(copies, derivs_hbm, grad_hbm, stats, derivs, sems, grad, grad_sems):
    rows = grad.shape[0] // copies
    waits = []
    grad_copies = []
    for c in range(copies):
        part = pl.ds(c * rows, rows)
        grad_copies.append(pltpu.make_async_copy(grad_hbm.at[part, :], grad.at[part, :], grad_sems.at[c]))
        grad_copies[-1].start()
        cols = pl.ds(c * rows * LANES, rows * LANES)
        waits.append(pltpu.make_async_copy(derivs_hbm.at[:, cols], derivs.at[:, cols], sems.at[c]))
        waits[-1].start()
    total = jnp.zeros((SUBLANES, LANES), jnp.float32)
    squares = total
    for c in range(copies):
        grad_copies[c].wait()
        waits[c].wait()
        total = total + products(derivs, grad, c * rows, rows)
        part = grad[c * rows : (c + 1) * rows, :]
        squares = squares + tile_sum(part * part)
    stats[0:8, :] = lane_total(total)
    stats[8:16, :] = all_total(squares)
    stats[16:24, :] = jnp.zeros((SUBLANES, LANES), jnp.float32)


def start_call(derivs, grad):
    rows = grad.shape[0]
    copies = whole_tiles(rows, COPIES)
    return pl.pallas_call(
        functools.partial(start_kernel, copies),
        in_specs=[hbm(), hbm()],
        out_specs=[vmem(), vmem()],
        out_shape=[jax.ShapeDtypeStruct((24, LANES), jnp.float32), pltpu.VMEM(derivs.shape, jnp.float32)],
        scratch_shapes=[
            pltpu.SemaphoreType.DMA((copies,)),
            pltpu.VMEM((rows, LANES), jnp.float32),
            pltpu.SemaphoreType.DMA((copies,)),
        ],
        compiler_params=pltpu.CompilerParams(vmem_limit_bytes=START_VMEM),
        cost_estimate=pl.CostEstimate(flops=0, bytes_accessed=0, transcendentals=0),
        name="start_products",
    )(pltpu.with_memory_space_constraint(derivs, pltpu.HBM), pltpu.with_memory_space_constraint(grad, pltpu.HBM))


def back_kernel(offset, derivs, vals_ref, out):
    vals = vals_ref[...]
    rows = out.shape[0] - EXTRA
    out[rows : rows + EXTRA, :] = jnp.broadcast_to(jnp.sum(vals * vals, axis=0, keepdims=True), (EXTRA, LANES))
    unroll = unroll_of(rows // SUBLANES)

    def step(i, carry):
        for u in range(unroll):
            row = (i * unroll + u) * SUBLANES
            tiles = [tile * vals for tile in eight_tiles(derivs, offset + row)]
            out[pl.ds(pl.multiple_of(row, SUBLANES), SUBLANES), :] = sublane_sums(tiles)
        return carry

    lax.fori_loop(0, rows // SUBLANES // unroll, step, 0)


def back_call(derivs, vals, chunk, rows):
    return pl.pallas_call(
        functools.partial(back_kernel, chunk * rows),
        in_specs=[vmem(), vmem()],
        out_specs=vmem(),
        out_shape=jax.ShapeDtypeStruct((rows + EXTRA, LANES), jnp.float32),
        compiler_params=pltpu.CompilerParams(vmem_limit_bytes=BACK_VMEM),
        cost_estimate=pl.CostEstimate(flops=0, bytes_accessed=0, transcendentals=0),
        name="back_products",
    )(pltpu.with_memory_space_constraint(derivs, pltpu.VMEM), vals)


def step_length(norm, squares, rows_all, dir_sq):
    return norm / (squares / rows_all + DAMPING * dir_sq)


def advance_kernel(offset, rows_all, last, derivs, back, squares, known, res, prev, stats_in, new, stats):
    rows = new.shape[0]
    norm, dir_sq, beta = known[0:1, :], known[1:2, :], known[2:3, :]
    step_len = step_length(norm, squares[0:1, :], rows_all, dir_sq)
    old = res[...]
    direction = old + beta * prev[...]
    fresh = old - step_len * (back[0:rows, :] * (1.0 / rows_all) + DAMPING * direction)
    new[...] = fresh
    norms = stats_in[8:16, :] + tile_sum(fresh * fresh)
    cross = stats_in[16:24, :] + tile_sum(fresh * direction)
    total = stats_in[0:8, :] + products(derivs, new, 0, rows, offset)
    if last:
        total, norms, cross = lane_total(total), all_total(norms), all_total(cross)
    stats[0:8, :] = total
    stats[8:16, :] = norms
    stats[16:24, :] = cross


def advance_call(derivs, back, first_back, known, residual, prev, stats, chunk, rows, rows_all, last):
    here = pl.BlockSpec((rows, LANES), lambda i: (0, 0))
    part = pl.BlockSpec((rows, LANES), lambda i: (chunk, 0))
    rest = pl.BlockSpec((EXTRA, LANES), lambda i: (rows // EXTRA, 0))
    tile = pl.BlockSpec((SUBLANES, LANES), lambda i: (0, 0))
    sums = pl.BlockSpec((24, LANES), lambda i: (0, 0))
    return pl.pallas_call(
        functools.partial(advance_kernel, chunk * rows, rows_all, last),
        grid=(1,),
        in_specs=[vmem(), here, rest, tile, here if residual.shape[0] == rows else part, part, sums],
        out_specs=[here, sums],
        out_shape=[
            jax.ShapeDtypeStruct((rows, LANES), jnp.float32),
            jax.ShapeDtypeStruct((24, LANES), jnp.float32),
        ],
        compiler_params=pltpu.CompilerParams(vmem_limit_bytes=ADVANCE_VMEM),
        cost_estimate=pl.CostEstimate(flops=0, bytes_accessed=0, transcendentals=0),
        name="advance_residual",
    )(pltpu.with_memory_space_constraint(derivs, pltpu.VMEM), back, first_back, known, residual, prev, stats)


def share_kernel(share_ref, grad_ref, res1_ref, res2_ref, coef_ref, base_ref, dir_ref, last_ref):
    step0, step1, beta1 = (coef_ref[i : i + 1, :] for i in range(3))
    direction1 = res1_ref[...] + beta1 * grad_ref[...]
    base_ref[...] = step0 * grad_ref[...] + step1 * direction1
    dir_ref[...] = direction1
    last_ref[...] = res2_ref[...]


def share_call(share, grad, res1, res2, coefs, share_rows):
    vec = pl.BlockSpec((share_rows, LANES), lambda i, share_ref: (share_ref[0], 0))
    out = pl.BlockSpec((share_rows, LANES), lambda i, share_ref: (0, 0))
    return pl.pallas_call(
        share_kernel,
        grid_spec=pltpu.PrefetchScalarGridSpec(
            num_scalar_prefetch=1,
            grid=(1,),
            in_specs=[vec, vec, vec, pl.BlockSpec((SUBLANES, LANES), lambda i, share_ref: (0, 0))],
            out_specs=[out] * 3,
        ),
        out_shape=[pltpu.VMEM((share_rows, LANES), jnp.float32)] * 3,
        cost_estimate=pl.CostEstimate(flops=0, bytes_accessed=24 * share_rows * LANES, transcendentals=0),
        name="share_parts",
    )(share, grad, res1, res2, coefs)


def small_sum(value, axis, beside=()):
    size = lax.axis_size(axis)
    if size & (size - 1):
        return lax.psum(value, axis), beside
    bit = 1
    while bit < size:
        if bit > 1 and beside:
            value, *beside = lax.optimization_barrier((value, *beside))
        fan = 2 if bit * 4 > size or (bit == 1 and size not in (4, 16)) else 4
        got = [lax.ppermute(value, axis, [(i, i ^ (bit * j)) for i in range(size)]) for j in range(1, fan)]
        if fan == 4:
            first = value + got[0]
            value = first + (got[1] + got[2])
        else:
            value = value + got[0]
        bit *= fan
    return value, tuple(beside)


def chain(chunks, produce, consume, state, gate):
    count = lax.axis_size("walker")
    me = lax.axis_index("walker")
    gaps = (2, 2)
    up, down = [0], [0]
    for link in range(count - 2):
        up.append(up[-1] + gaps[link % 2])
    for link in range(count - 2, 0, -1):
        down.insert(0, down[0] + gaps[link % 2])

    def links(parity):
        partner, send, recv = {}, {}, {}
        for w in range(count):
            other = w + 1 if w % 2 == parity else w - 1
            if 0 <= other < count:
                link = min(w, other)
                partner[w] = other
                send[w], recv[w] = (up[link], down[link]) if other > w else (down[link], up[link])
        return partner, send, recv

    def pick(items, at, delays):
        found = None
        for delay in sorted(set(delays.values())):
            if not 0 <= at - delay < len(items) or items[at - delay] is None:
                continue
            if found is None:
                found = items[at - delay]
            else:
                mine = functools.reduce(jnp.logical_or, [me == w for w in delays if delays[w] == delay])
                found = jnp.where(mine, items[at - delay], found)
        return found

    both = (links(0), links(1))
    made = [produce(0, gate)]
    got = ([], [])

    def complete(chunk):
        total = made[chunk]
        for parity, (_, _, recv) in enumerate(both):
            arrived = pick(got[parity], chunk, {w: -delay for w, delay in recv.items()})
            if arrived is not None:
                total = total + arrived
        return total

    def exchange(parity, step, before, gate, state):
        partner, send, _ = both[parity]
        pairs = [(w, partner[w]) for w in partner if 0 <= step - send[w] < chunks]
        own = pick(made, step, send) if pairs else None
        if own is None:
            got[parity].append(None)
            return gate, state
        if 0 <= before < step and got[1 - parity][before] is not None:
            own = own + got[1 - parity][before]
        own, gate, *state = lax.optimization_barrier((own, gate, *state))
        got[parity].append(lax.ppermute(own, "walker", pairs))
        return gate, tuple(state)

    late = [max(recv.values(), default=-1) for _, _, recv in both]
    lag = 1 + max(late[0], late[1] + 1)
    steps = chunks + max(late)
    for step in range(steps):
        gate, state = exchange(0, step, step - gaps[1], gate, state)
        if step + 1 < chunks:
            made.append(produce(step + 1, gate))
            made[-1], gate, *state = lax.optimization_barrier((made[-1], gate, *state))
            state = tuple(state)
        gate, state = exchange(1, step, step - gaps[0], gate, state)
        if step - lag >= 0:
            state = consume(step - lag, complete(step - lag), state)
    for chunk in range(max(steps - lag, 0), chunks):
        state = consume(chunk, complete(chunk), state)
    return state


def body(derivs, gradient):
    walkers = lax.axis_size("walker")
    rows_all = derivs.shape[0] * walkers
    rows = gradient.shape[0] // LANES
    grad = gradient.reshape(rows, LANES)
    chunks = whole_tiles(rows, CHUNKS)
    part = rows // chunks

    def advance(residual, prev, vals, norm, dir_sq, beta):
        known = jnp.concatenate([norm, dir_sq, beta, jnp.zeros((5, LANES), jnp.float32)])
        first = []
        fresh = []

        def consume(chunk, total, state):
            if not first:
                first.append(total)
            last = chunk == chunks - 1
            old = residual[chunk] if isinstance(residual, list) else residual
            new, stats = advance_call(
                derivs, total, first[0], known, old, prev, state[0], chunk, part, rows_all, last
            )
            fresh.append(new)
            return (stats,)

        def produce(chunk, gate):
            return back_call(derivs, gate, chunk, part)

        state = (jnp.zeros((24, LANES), jnp.float32),)
        (stats,) = chain(chunks, produce, consume, state, vals)
        step = step_length(norm, first[0][part : part + 1], rows_all, dir_sq)
        return fresh, step, stats

    stats, derivs = start_call(derivs, grad)
    stats, _ = small_sum(stats, "param")
    vals0, norm0 = stats[0:8], stats[8:9]
    dir_sq0 = norm0
    res1, step0, stats = advance(grad, grad, vals0, norm0, dir_sq0, jnp.zeros_like(norm0))

    stats, _ = small_sum(stats, "param")

    norm1, cross1 = stats[8:9], stats[16:17]
    beta1 = norm1 / norm0
    vals1 = stats[0:8] + beta1 * vals0
    dir_sq1 = norm1 + 2.0 * beta1 * cross1 + beta1 * beta1 * dir_sq0
    res2, step1, stats = advance(res1, grad, vals1, norm1, dir_sq1, beta1)

    coefs = jnp.concatenate([step0, step1, beta1, jnp.zeros((5, LANES), jnp.float32)])
    whole1, whole2 = jnp.concatenate(res1), jnp.concatenate(res2)
    stats, (whole1, whole2, coefs) = small_sum(stats, "param", (whole1, whole2, coefs))
    share = lax.axis_index("walker").astype(jnp.int32).reshape(1)
    base, direction1, res = share_call(share, grad, whole1, whole2, coefs, rows // walkers)

    norm2, cross2 = stats[8:9], stats[16:17]
    beta2 = norm2 / norm1
    vals2 = stats[0:8] + beta2 * vals1
    dir_sq2 = norm2 + 2.0 * beta2 * cross2 + beta2 * beta2 * dir_sq1
    squares, _ = small_sum(jnp.sum(vals2 * vals2, axis=0, keepdims=True), "walker")
    step2 = step_length(norm2, squares, rows_all, dir_sq2)
    return (base + step2 * (res + beta2 * direction1)).reshape(-1)


def solution(mesh):
    in_specs = (P("walker", "param"), P("param"))
    out_specs = P(("param", "walker"))
    return jax.shard_map(body, mesh=mesh, in_specs=in_specs, out_specs=out_specs, check_vma=False)
```

```python
import functools

import jax
import jax.numpy as jnp
from jax import lax
from jax.experimental import pallas as pl
from jax.experimental.pallas import tpu as pltpu
from jax.sharding import PartitionSpec as P

DAMPING = 0.001
LANES = 128
SUBLANES = 8
CHUNKS = 8
COPIES = 8
START_VMEM = 3 * 2**20
BACK_VMEM = 1 * 2**20
ADVANCE_VMEM = 3 * 2**20
EXTRA = 8


def whole_tiles(rows, parts):
    return max(n for n in range(1, parts + 1) if rows % (n * SUBLANES) == 0)


def unroll_of(groups):
    return max(u for u in (1, 2, 4) if groups % u == 0)


def lane_total(tile):
    return jnp.broadcast_to(jnp.sum(tile, axis=1, keepdims=True), tile.shape)


def all_total(tile):
    return lane_total(jnp.broadcast_to(jnp.sum(tile, axis=0, keepdims=True), tile.shape))


def tile_sum(block):
    return jnp.sum(block.reshape(-1, SUBLANES, LANES), axis=0)


def eight_tiles(derivs, row):
    width = SUBLANES * LANES
    block = derivs[:, pl.ds(pl.multiple_of(row * LANES, width), width)]
    return [block[:, s * LANES : (s + 1) * LANES] for s in range(SUBLANES)]


def products(derivs, vec, first, rows, offset=0):
    unroll = unroll_of(rows // SUBLANES)

    def step(i, accs):
        accs = list(accs)
        for u in range(unroll):
            row = first + (i * unroll + u) * SUBLANES
            vals = vec[pl.ds(pl.multiple_of(row, SUBLANES), SUBLANES), :]
            tiles = eight_tiles(derivs, offset + row)
            for s in range(SUBLANES):
                accs[s] = accs[s] + tiles[s] * jnp.broadcast_to(vals[s : s + 1, :], (SUBLANES, LANES))
        return tuple(accs)

    zero = jnp.zeros((SUBLANES, LANES), jnp.float32)
    a = lax.fori_loop(0, rows // SUBLANES // unroll, step, (zero,) * SUBLANES)
    return ((a[0] + a[1]) + (a[2] + a[3])) + ((a[4] + a[5]) + (a[6] + a[7]))


def sublane_sums(tiles):
    index = lax.broadcasted_iota(jnp.int32, (SUBLANES, LANES), 0)
    half = SUBLANES // 2
    while half >= 1:
        low = (index & half) == 0
        merged = []
        for s in range(half):
            a, b = tiles[s], tiles[s + half]
            keep, move = jnp.where(low, a, b), jnp.where(low, b, a)
            if half == SUBLANES // 2:
                moved = pltpu.roll(move, half, 0)
            else:
                moved = jnp.where(low, pltpu.roll(move, SUBLANES - half, 0), pltpu.roll(move, half, 0))
            merged.append(keep + moved)
        tiles = merged
        half //= 2
    return tiles[0]


def vmem():
    return pl.BlockSpec(memory_space=pltpu.VMEM)


def hbm():
    return pl.BlockSpec(memory_space=pltpu.HBM)


def start_kernel(copies, derivs_hbm, grad_hbm, stats, derivs, sems, grad, grad_sems):
    rows = grad.shape[0] // copies
    waits = []
    grad_copies = []
    for c in range(copies):
        part = pl.ds(c * rows, rows)
        grad_copies.append(pltpu.make_async_copy(grad_hbm.at[part, :], grad.at[part, :], grad_sems.at[c]))
        grad_copies[-1].start()
        cols = pl.ds(c * rows * LANES, rows * LANES)
        waits.append(pltpu.make_async_copy(derivs_hbm.at[:, cols], derivs.at[:, cols], sems.at[c]))
        waits[-1].start()
    total = jnp.zeros((SUBLANES, LANES), jnp.float32)
    squares = total
    for c in range(copies):
        grad_copies[c].wait()
        waits[c].wait()
        total = total + products(derivs, grad, c * rows, rows)
        part = grad[c * rows : (c + 1) * rows, :]
        squares = squares + tile_sum(part * part)
    stats[0:8, :] = lane_total(total)
    stats[8:16, :] = all_total(squares)
    stats[16:24, :] = jnp.zeros((SUBLANES, LANES), jnp.float32)


def start_call(derivs, grad):
    rows = grad.shape[0]
    copies = whole_tiles(rows, COPIES)
    return pl.pallas_call(
        functools.partial(start_kernel, copies),
        in_specs=[hbm(), hbm()],
        out_specs=[vmem(), vmem()],
        out_shape=[jax.ShapeDtypeStruct((24, LANES), jnp.float32), pltpu.VMEM(derivs.shape, jnp.float32)],
        scratch_shapes=[
            pltpu.SemaphoreType.DMA((copies,)),
            pltpu.VMEM((rows, LANES), jnp.float32),
            pltpu.SemaphoreType.DMA((copies,)),
        ],
        compiler_params=pltpu.CompilerParams(vmem_limit_bytes=START_VMEM),
        cost_estimate=pl.CostEstimate(flops=0, bytes_accessed=0, transcendentals=0),
        name="start_products",
    )(pltpu.with_memory_space_constraint(derivs, pltpu.HBM), pltpu.with_memory_space_constraint(grad, pltpu.HBM))


def back_kernel(offset, derivs, vals_ref, out):
    vals = vals_ref[...]
    rows = out.shape[0] - EXTRA
    out[rows : rows + EXTRA, :] = jnp.broadcast_to(jnp.sum(vals * vals, axis=0, keepdims=True), (EXTRA, LANES))
    unroll = unroll_of(rows // SUBLANES)

    def step(i, carry):
        for u in range(unroll):
            row = (i * unroll + u) * SUBLANES
            tiles = [tile * vals for tile in eight_tiles(derivs, offset + row)]
            out[pl.ds(pl.multiple_of(row, SUBLANES), SUBLANES), :] = sublane_sums(tiles)
        return carry

    lax.fori_loop(0, rows // SUBLANES // unroll, step, 0)


def back_call(derivs, vals, chunk, rows):
    return pl.pallas_call(
        functools.partial(back_kernel, chunk * rows),
        in_specs=[vmem(), vmem()],
        out_specs=vmem(),
        out_shape=jax.ShapeDtypeStruct((rows + EXTRA, LANES), jnp.float32),
        compiler_params=pltpu.CompilerParams(vmem_limit_bytes=BACK_VMEM),
        cost_estimate=pl.CostEstimate(flops=0, bytes_accessed=0, transcendentals=0),
        name="back_products",
    )(pltpu.with_memory_space_constraint(derivs, pltpu.VMEM), vals)


def step_length(norm, squares, rows_all, dir_sq):
    return norm / (squares / rows_all + DAMPING * dir_sq)


def advance_kernel(offset, rows_all, last, derivs, back, squares, known, res, prev, stats_in, new, stats):
    rows = new.shape[0]
    norm, dir_sq, beta = known[0:1, :], known[1:2, :], known[2:3, :]
    step_len = step_length(norm, squares[0:1, :], rows_all, dir_sq)
    old = res[...]
    direction = old + beta * prev[...]
    fresh = old - step_len * (back[0:rows, :] * (1.0 / rows_all) + DAMPING * direction)
    new[...] = fresh
    norms = stats_in[8:16, :] + tile_sum(fresh * fresh)
    cross = stats_in[16:24, :] + tile_sum(fresh * direction)
    total = stats_in[0:8, :] + products(derivs, new, 0, rows, offset)
    if last:
        total, norms, cross = lane_total(total), all_total(norms), all_total(cross)
    stats[0:8, :] = total
    stats[8:16, :] = norms
    stats[16:24, :] = cross


def advance_call(derivs, back, first_back, known, residual, prev, stats, chunk, rows, rows_all, last):
    here = pl.BlockSpec((rows, LANES), lambda i: (0, 0))
    part = pl.BlockSpec((rows, LANES), lambda i: (chunk, 0))
    rest = pl.BlockSpec((EXTRA, LANES), lambda i: (rows // EXTRA, 0))
    tile = pl.BlockSpec((SUBLANES, LANES), lambda i: (0, 0))
    sums = pl.BlockSpec((24, LANES), lambda i: (0, 0))
    return pl.pallas_call(
        functools.partial(advance_kernel, chunk * rows, rows_all, last),
        grid=(1,),
        in_specs=[vmem(), here, rest, tile, here if residual.shape[0] == rows else part, part, sums],
        out_specs=[here, sums],
        out_shape=[
            jax.ShapeDtypeStruct((rows, LANES), jnp.float32),
            jax.ShapeDtypeStruct((24, LANES), jnp.float32),
        ],
        compiler_params=pltpu.CompilerParams(vmem_limit_bytes=ADVANCE_VMEM),
        cost_estimate=pl.CostEstimate(flops=0, bytes_accessed=0, transcendentals=0),
        name="advance_residual",
    )(pltpu.with_memory_space_constraint(derivs, pltpu.VMEM), back, first_back, known, residual, prev, stats)


def share_kernel(share_ref, grad_ref, res1_ref, res2_ref, coef_ref, base_ref, dir_ref, last_ref):
    step0, step1, beta1 = (coef_ref[i : i + 1, :] for i in range(3))
    direction1 = res1_ref[...] + beta1 * grad_ref[...]
    base_ref[...] = step0 * grad_ref[...] + step1 * direction1
    dir_ref[...] = direction1
    last_ref[...] = res2_ref[...]


def share_call(share, grad, res1, res2, coefs, share_rows):
    vec = pl.BlockSpec((share_rows, LANES), lambda i, share_ref: (share_ref[0], 0))
    out = pl.BlockSpec((share_rows, LANES), lambda i, share_ref: (0, 0))
    return pl.pallas_call(
        share_kernel,
        grid_spec=pltpu.PrefetchScalarGridSpec(
            num_scalar_prefetch=1,
            grid=(1,),
            in_specs=[vec, vec, vec, pl.BlockSpec((SUBLANES, LANES), lambda i, share_ref: (0, 0))],
            out_specs=[out] * 3,
        ),
        out_shape=[pltpu.VMEM((share_rows, LANES), jnp.float32)] * 3,
        cost_estimate=pl.CostEstimate(flops=0, bytes_accessed=24 * share_rows * LANES, transcendentals=0),
        name="share_parts",
    )(share, grad, res1, res2, coefs)


def small_sum(value, axis, beside=()):
    size = lax.axis_size(axis)
    if size & (size - 1):
        return lax.psum(value, axis), beside
    bit = 1
    while bit < size:
        if bit > 1 and beside:
            value, *beside = lax.optimization_barrier((value, *beside))
        fan = 2 if bit * 4 > size or (bit == 1 and size not in (4, 16)) else 4
        got = [lax.ppermute(value, axis, [(i, i ^ (bit * j)) for i in range(size)]) for j in range(1, fan)]
        if fan == 4:
            first = value + got[0]
            value = first + (got[1] + got[2])
        else:
            value = value + got[0]
        bit *= fan
    return value, tuple(beside)


def chain(chunks, produce, consume, state, gate, eager):
    count = lax.axis_size("walker")
    me = lax.axis_index("walker")
    gaps = (2, 2)
    up, down = [0], [0]
    for link in range(count - 2):
        up.append(up[-1] + gaps[link % 2])
    for link in range(count - 2, 0, -1):
        down.insert(0, down[0] + gaps[link % 2])

    def links(parity):
        partner, send, recv = {}, {}, {}
        for w in range(count):
            other = w + 1 if w % 2 == parity else w - 1
            if 0 <= other < count:
                link = min(w, other)
                partner[w] = other
                send[w], recv[w] = (up[link], down[link]) if other > w else (down[link], up[link])
        return partner, send, recv

    def pick(items, at, delays):
        found = None
        for delay in sorted(set(delays.values())):
            if not 0 <= at - delay < len(items) or items[at - delay] is None:
                continue
            if found is None:
                found = items[at - delay]
            else:
                mine = functools.reduce(jnp.logical_or, [me == w for w in delays if delays[w] == delay])
                found = jnp.where(mine, items[at - delay], found)
        return found

    both = (links(0), links(1))
    made = [produce(0, gate)]
    got = ([], [])

    def complete(chunk):
        total = made[chunk]
        for parity, (_, _, recv) in enumerate(both):
            arrived = pick(got[parity], chunk, {w: -delay for w, delay in recv.items()})
            if arrived is not None:
                total = total + arrived
        return total

    def exchange(parity, step, before, gate, state):
        partner, send, _ = both[parity]
        pairs = [(w, partner[w]) for w in partner if 0 <= step - send[w] < chunks]
        own = pick(made, step, send) if pairs else None
        if own is None:
            got[parity].append(None)
            return gate, state
        if 0 <= before < step and got[1 - parity][before] is not None:
            own = own + got[1 - parity][before]
        own, gate, *state = lax.optimization_barrier((own, gate, *state))
        got[parity].append(lax.ppermute(own, "walker", pairs))
        return gate, tuple(state)

    late = [max(recv.values(), default=-1) for _, _, recv in both]
    lag = 1 + max(late[0], late[1] + 1)
    steps = chunks + max(late)
    for step in range(steps):
        gate, state = exchange(0, step, step - gaps[1], gate, state)
        if step == 0 and eager:
            made += [produce(chunk, gate) for chunk in range(1, chunks)]
            *made[1:], gate = lax.optimization_barrier((*made[1:], gate))
        if len(made) < chunks and not eager:
            made.append(produce(step + 1, gate))
            made[-1], gate, *state = lax.optimization_barrier((made[-1], gate, *state))
            state = tuple(state)
        gate, state = exchange(1, step, step - gaps[0], gate, state)
        if step - lag >= 0:
            state = consume(step - lag, complete(step - lag), state)
    for chunk in range(max(steps - lag, 0), chunks):
        state = consume(chunk, complete(chunk), state)
    return state


def body(derivs, gradient):
    walkers = lax.axis_size("walker")
    rows_all = derivs.shape[0] * walkers
    rows = gradient.shape[0] // LANES
    grad = gradient.reshape(rows, LANES)
    chunks = whole_tiles(rows, CHUNKS)
    part = rows // chunks

    def advance(residual, prev, vals, norm, dir_sq, beta):
        known = jnp.concatenate([norm, dir_sq, beta, jnp.zeros((5, LANES), jnp.float32)])
        first = []
        fresh = []

        def consume(chunk, total, state):
            if not first:
                first.append(total)
            last = chunk == chunks - 1
            old = residual[chunk] if isinstance(residual, list) else residual
            new, stats = advance_call(
                derivs, total, first[0], known, old, prev, state[0], chunk, part, rows_all, last
            )
            fresh.append(new)
            return (stats,)

        def produce(chunk, gate):
            return back_call(derivs, gate, chunk, part)

        state = (jnp.zeros((24, LANES), jnp.float32),)
        (stats,) = chain(chunks, produce, consume, state, vals, isinstance(residual, list))
        step = step_length(norm, first[0][part : part + 1], rows_all, dir_sq)
        return fresh, step, stats

    stats, derivs = start_call(derivs, grad)
    stats, _ = small_sum(stats, "param")
    vals0, norm0 = stats[0:8], stats[8:9]
    dir_sq0 = norm0
    res1, step0, stats = advance(grad, grad, vals0, norm0, dir_sq0, jnp.zeros_like(norm0))

    stats, _ = small_sum(stats, "param")

    norm1, cross1 = stats[8:9], stats[16:17]
    beta1 = norm1 / norm0
    vals1 = stats[0:8] + beta1 * vals0
    dir_sq1 = norm1 + 2.0 * beta1 * cross1 + beta1 * beta1 * dir_sq0
    res2, step1, stats = advance(res1, grad, vals1, norm1, dir_sq1, beta1)

    coefs = jnp.concatenate([step0, step1, beta1, jnp.zeros((5, LANES), jnp.float32)])
    whole1, whole2 = jnp.concatenate(res1), jnp.concatenate(res2)
    stats, (whole1, whole2, coefs) = small_sum(stats, "param", (whole1, whole2, coefs))
    share = lax.axis_index("walker").astype(jnp.int32).reshape(1)
    base, direction1, res = share_call(share, grad, whole1, whole2, coefs, rows // walkers)
    stats, base, direction1, res = lax.optimization_barrier((stats, base, direction1, res))

    norm2, cross2 = stats[8:9], stats[16:17]
    beta2 = norm2 / norm1
    vals2 = stats[0:8] + beta2 * vals1
    dir_sq2 = norm2 + 2.0 * beta2 * cross2 + beta2 * beta2 * dir_sq1
    squares, _ = small_sum(jnp.sum(vals2 * vals2, axis=0, keepdims=True), "walker")
    step2 = step_length(norm2, squares, rows_all, dir_sq2)
    return (base + step2 * (res + beta2 * direction1)).reshape(-1)


def solution(mesh):
    in_specs = (P("walker", "param"), P("param"))
    out_specs = P(("param", "walker"))
    return jax.shard_map(body, mesh=mesh, in_specs=in_specs, out_specs=out_specs, check_vma=False)
```

```python
import functools

import jax
import jax.numpy as jnp
from jax import lax
from jax.experimental import pallas as pl
from jax.experimental.pallas import tpu as pltpu
from jax.sharding import PartitionSpec as P

DAMPING = 0.001
LANES = 128
SUBLANES = 8
CHUNKS = 8
COPIES = 8
START_VMEM = 3 * 2**20
BACK_VMEM = 1 * 2**20
ADVANCE_VMEM = 3 * 2**20
EXTRA = 8


def whole_tiles(rows, parts):
    return max(n for n in range(1, parts + 1) if rows % (n * SUBLANES) == 0)


def unroll_of(groups):
    return max(u for u in (1, 2, 4) if groups % u == 0)


def lane_total(tile):
    return jnp.broadcast_to(jnp.sum(tile, axis=1, keepdims=True), tile.shape)


def all_total(tile):
    return lane_total(jnp.broadcast_to(jnp.sum(tile, axis=0, keepdims=True), tile.shape))


def tile_sum(block):
    return jnp.sum(block.reshape(-1, SUBLANES, LANES), axis=0)


def eight_tiles(derivs, row):
    width = SUBLANES * LANES
    block = derivs[:, pl.ds(pl.multiple_of(row * LANES, width), width)]
    return [block[:, s * LANES : (s + 1) * LANES] for s in range(SUBLANES)]


def products(derivs, vec, first, rows, offset=0):
    unroll = unroll_of(rows // SUBLANES)

    def step(i, accs):
        accs = list(accs)
        for u in range(unroll):
            row = first + (i * unroll + u) * SUBLANES
            vals = vec[pl.ds(pl.multiple_of(row, SUBLANES), SUBLANES), :]
            tiles = eight_tiles(derivs, offset + row)
            for s in range(SUBLANES):
                accs[s] = accs[s] + tiles[s] * jnp.broadcast_to(vals[s : s + 1, :], (SUBLANES, LANES))
        return tuple(accs)

    zero = jnp.zeros((SUBLANES, LANES), jnp.float32)
    a = lax.fori_loop(0, rows // SUBLANES // unroll, step, (zero,) * SUBLANES)
    return ((a[0] + a[1]) + (a[2] + a[3])) + ((a[4] + a[5]) + (a[6] + a[7]))


def sublane_sums(tiles):
    index = lax.broadcasted_iota(jnp.int32, (SUBLANES, LANES), 0)
    half = SUBLANES // 2
    while half >= 1:
        low = (index & half) == 0
        merged = []
        for s in range(half):
            a, b = tiles[s], tiles[s + half]
            keep, move = jnp.where(low, a, b), jnp.where(low, b, a)
            if half == SUBLANES // 2:
                moved = pltpu.roll(move, half, 0)
            else:
                moved = jnp.where(low, pltpu.roll(move, SUBLANES - half, 0), pltpu.roll(move, half, 0))
            merged.append(keep + moved)
        tiles = merged
        half //= 2
    return tiles[0]


def vmem():
    return pl.BlockSpec(memory_space=pltpu.VMEM)


def hbm():
    return pl.BlockSpec(memory_space=pltpu.HBM)


def start_kernel(copies, derivs_hbm, grad_hbm, stats, derivs, sems, grad, grad_sems):
    rows = grad.shape[0] // copies
    waits = []
    grad_copies = []
    for c in range(copies):
        part = pl.ds(c * rows, rows)
        grad_copies.append(pltpu.make_async_copy(grad_hbm.at[part, :], grad.at[part, :], grad_sems.at[c]))
        grad_copies[-1].start()
        cols = pl.ds(c * rows * LANES, rows * LANES)
        waits.append(pltpu.make_async_copy(derivs_hbm.at[:, cols], derivs.at[:, cols], sems.at[c]))
        waits[-1].start()
    total = jnp.zeros((SUBLANES, LANES), jnp.float32)
    squares = total
    for c in range(copies):
        grad_copies[c].wait()
        waits[c].wait()
        total = total + products(derivs, grad, c * rows, rows)
        part = grad[c * rows : (c + 1) * rows, :]
        squares = squares + tile_sum(part * part)
    stats[0:8, :] = lane_total(total)
    stats[8:16, :] = all_total(squares)
    stats[16:24, :] = jnp.zeros((SUBLANES, LANES), jnp.float32)


def start_call(derivs, grad):
    rows = grad.shape[0]
    copies = whole_tiles(rows, COPIES)
    return pl.pallas_call(
        functools.partial(start_kernel, copies),
        in_specs=[hbm(), hbm()],
        out_specs=[vmem(), vmem()],
        out_shape=[jax.ShapeDtypeStruct((24, LANES), jnp.float32), pltpu.VMEM(derivs.shape, jnp.float32)],
        scratch_shapes=[
            pltpu.SemaphoreType.DMA((copies,)),
            pltpu.VMEM((rows, LANES), jnp.float32),
            pltpu.SemaphoreType.DMA((copies,)),
        ],
        compiler_params=pltpu.CompilerParams(vmem_limit_bytes=START_VMEM),
        cost_estimate=pl.CostEstimate(flops=0, bytes_accessed=0, transcendentals=0),
        name="start_products",
    )(pltpu.with_memory_space_constraint(derivs, pltpu.HBM), pltpu.with_memory_space_constraint(grad, pltpu.HBM))


def back_kernel(offset, derivs, vals_ref, out):
    vals = vals_ref[...]
    rows = out.shape[0] - EXTRA
    out[rows : rows + EXTRA, :] = jnp.broadcast_to(jnp.sum(vals * vals, axis=0, keepdims=True), (EXTRA, LANES))
    unroll = unroll_of(rows // SUBLANES)

    def step(i, carry):
        for u in range(unroll):
            row = (i * unroll + u) * SUBLANES
            tiles = [tile * vals for tile in eight_tiles(derivs, offset + row)]
            out[pl.ds(pl.multiple_of(row, SUBLANES), SUBLANES), :] = sublane_sums(tiles)
        return carry

    lax.fori_loop(0, rows // SUBLANES // unroll, step, 0)


def back_call(derivs, vals, chunk, rows):
    return pl.pallas_call(
        functools.partial(back_kernel, chunk * rows),
        in_specs=[vmem(), vmem()],
        out_specs=vmem(),
        out_shape=jax.ShapeDtypeStruct((rows + EXTRA, LANES), jnp.float32),
        compiler_params=pltpu.CompilerParams(vmem_limit_bytes=BACK_VMEM),
        cost_estimate=pl.CostEstimate(flops=0, bytes_accessed=0, transcendentals=0),
        name="back_products",
    )(pltpu.with_memory_space_constraint(derivs, pltpu.VMEM), vals)


def step_length(norm, squares, rows_all, dir_sq):
    return norm / (squares / rows_all + DAMPING * dir_sq)


def advance_kernel(offset, rows_all, last, derivs, back, squares, known, res, prev, stats_in, new, stats):
    rows = new.shape[0]
    norm, dir_sq, beta = known[0:1, :], known[1:2, :], known[2:3, :]
    step_len = step_length(norm, squares[0:1, :], rows_all, dir_sq)
    old = res[...]
    direction = old + beta * prev[...]
    fresh = old - step_len * (back[0:rows, :] * (1.0 / rows_all) + DAMPING * direction)
    new[...] = fresh
    norms = stats_in[8:16, :] + tile_sum(fresh * fresh)
    cross = stats_in[16:24, :] + tile_sum(fresh * direction)
    total = stats_in[0:8, :] + products(derivs, new, 0, rows, offset)
    if last:
        total, norms, cross = lane_total(total), all_total(norms), all_total(cross)
    stats[0:8, :] = total
    stats[8:16, :] = norms
    stats[16:24, :] = cross


def advance_call(derivs, back, first_back, known, residual, prev, stats, chunk, rows, rows_all, last):
    here = pl.BlockSpec((rows, LANES), lambda i: (0, 0))
    part = pl.BlockSpec((rows, LANES), lambda i: (chunk, 0))
    rest = pl.BlockSpec((EXTRA, LANES), lambda i: (rows // EXTRA, 0))
    tile = pl.BlockSpec((SUBLANES, LANES), lambda i: (0, 0))
    sums = pl.BlockSpec((24, LANES), lambda i: (0, 0))
    return pl.pallas_call(
        functools.partial(advance_kernel, chunk * rows, rows_all, last),
        grid=(1,),
        in_specs=[vmem(), here, rest, tile, here if residual.shape[0] == rows else part, part, sums],
        out_specs=[here, sums],
        out_shape=[
            jax.ShapeDtypeStruct((rows, LANES), jnp.float32),
            jax.ShapeDtypeStruct((24, LANES), jnp.float32),
        ],
        compiler_params=pltpu.CompilerParams(vmem_limit_bytes=ADVANCE_VMEM),
        cost_estimate=pl.CostEstimate(flops=0, bytes_accessed=0, transcendentals=0),
        name="advance_residual",
    )(pltpu.with_memory_space_constraint(derivs, pltpu.VMEM), back, first_back, known, residual, prev, stats)


def share_kernel(share_ref, grad_ref, res1_ref, res2_ref, coef_ref, base_ref, dir_ref, last_ref):
    step0, step1, beta1 = (coef_ref[i : i + 1, :] for i in range(3))
    direction1 = res1_ref[...] + beta1 * grad_ref[...]
    base_ref[...] = step0 * grad_ref[...] + step1 * direction1
    dir_ref[...] = direction1
    last_ref[...] = res2_ref[...]


def share_call(share, grad, res1, res2, coefs, share_rows):
    vec = pl.BlockSpec((share_rows, LANES), lambda i, share_ref: (share_ref[0], 0))
    out = pl.BlockSpec((share_rows, LANES), lambda i, share_ref: (0, 0))
    return pl.pallas_call(
        share_kernel,
        grid_spec=pltpu.PrefetchScalarGridSpec(
            num_scalar_prefetch=1,
            grid=(1,),
            in_specs=[vec, vec, vec, pl.BlockSpec((SUBLANES, LANES), lambda i, share_ref: (0, 0))],
            out_specs=[out] * 3,
        ),
        out_shape=[pltpu.VMEM((share_rows, LANES), jnp.float32)] * 3,
        cost_estimate=pl.CostEstimate(flops=0, bytes_accessed=24 * share_rows * LANES, transcendentals=0),
        name="share_parts",
    )(share, grad, res1, res2, coefs)


def small_sum(value, axis, beside=()):
    size = lax.axis_size(axis)
    if size & (size - 1):
        return lax.psum(value, axis), beside
    bit = 1
    while bit < size:
        if bit > 1 and beside:
            value, *beside = lax.optimization_barrier((value, *beside))
        fan = 2 if bit * 4 > size or (bit == 1 and size not in (4, 16)) else 4
        got = [lax.ppermute(value, axis, [(i, i ^ (bit * j)) for i in range(size)]) for j in range(1, fan)]
        if fan == 4:
            first = value + got[0]
            value = first + (got[1] + got[2])
        else:
            value = value + got[0]
        bit *= fan
    return value, tuple(beside)


def chain(chunks, produce, consume, state, gate, eager):
    count = lax.axis_size("walker")
    me = lax.axis_index("walker")
    gaps = (2, 2)
    up, down = [0], [0]
    for link in range(count - 2):
        up.append(up[-1] + gaps[link % 2])
    for link in range(count - 2, 0, -1):
        down.insert(0, down[0] + gaps[link % 2])

    def links(parity):
        partner, send, recv = {}, {}, {}
        for w in range(count):
            other = w + 1 if w % 2 == parity else w - 1
            if 0 <= other < count:
                link = min(w, other)
                partner[w] = other
                send[w], recv[w] = (up[link], down[link]) if other > w else (down[link], up[link])
        return partner, send, recv

    def pick(items, at, delays):
        found = None
        for delay in sorted(set(delays.values())):
            if not 0 <= at - delay < len(items) or items[at - delay] is None:
                continue
            if found is None:
                found = items[at - delay]
            else:
                mine = functools.reduce(jnp.logical_or, [me == w for w in delays if delays[w] == delay])
                found = jnp.where(mine, items[at - delay], found)
        return found

    both = (links(0), links(1))
    made = [produce(0, gate)]
    got = ([], [])

    def complete(chunk):
        total = made[chunk]
        for parity, (_, _, recv) in enumerate(both):
            arrived = pick(got[parity], chunk, {w: -delay for w, delay in recv.items()})
            if arrived is not None:
                total = total + arrived
        return total

    def exchange(parity, step, before, gate, state):
        partner, send, _ = both[parity]
        pairs = [(w, partner[w]) for w in partner if 0 <= step - send[w] < chunks]
        own = pick(made, step, send) if pairs else None
        if own is None:
            got[parity].append(None)
            return gate, state
        if 0 <= before < step and got[1 - parity][before] is not None:
            own = own + got[1 - parity][before]
        own, gate, *state = lax.optimization_barrier((own, gate, *state))
        got[parity].append(lax.ppermute(own, "walker", pairs))
        return gate, tuple(state)

    late = [max(recv.values(), default=-1) for _, _, recv in both]
    lag = 1 + max(late[0], late[1] + 1)
    steps = chunks + max(late)
    for step in range(steps):
        gate, state = exchange(0, step, step - gaps[1], gate, state)
        if step == 0 and eager:
            made += [produce(chunk, gate) for chunk in range(1, min(6, chunks))]
            *made[1:], gate = lax.optimization_barrier((*made[1:], gate))
        if len(made) < chunks and (step or not eager):
            made.append(produce(len(made), gate))
            made[-1], gate, *state = lax.optimization_barrier((made[-1], gate, *state))
            state = tuple(state)
        gate, state = exchange(1, step, step - gaps[0], gate, state)
        if step - lag >= 0:
            state = consume(step - lag, complete(step - lag), state)
    for chunk in range(max(steps - lag, 0), chunks):
        state = consume(chunk, complete(chunk), state)
    return state


def body(derivs, gradient):
    walkers = lax.axis_size("walker")
    rows_all = derivs.shape[0] * walkers
    rows = gradient.shape[0] // LANES
    grad = gradient.reshape(rows, LANES)
    chunks = whole_tiles(rows, CHUNKS)
    part = rows // chunks

    def advance(residual, prev, vals, norm, dir_sq, beta):
        known = jnp.concatenate([norm, dir_sq, beta, jnp.zeros((5, LANES), jnp.float32)])
        first = []
        fresh = []

        def consume(chunk, total, state):
            if not first:
                first.append(total)
            last = chunk == chunks - 1
            old = residual[chunk] if isinstance(residual, list) else residual
            new, stats = advance_call(
                derivs, total, first[0], known, old, prev, state[0], chunk, part, rows_all, last
            )
            fresh.append(new)
            return (stats,)

        def produce(chunk, gate):
            return back_call(derivs, gate, chunk, part)

        state = (jnp.zeros((24, LANES), jnp.float32),)
        (stats,) = chain(chunks, produce, consume, state, vals, isinstance(residual, list))
        step = step_length(norm, first[0][part : part + 1], rows_all, dir_sq)
        return fresh, step, stats

    stats, derivs = start_call(derivs, grad)
    stats, _ = small_sum(stats, "param")
    vals0, norm0 = stats[0:8], stats[8:9]
    dir_sq0 = norm0
    res1, step0, stats = advance(grad, grad, vals0, norm0, dir_sq0, jnp.zeros_like(norm0))

    stats, _ = small_sum(stats, "param")

    norm1, cross1 = stats[8:9], stats[16:17]
    beta1 = norm1 / norm0
    vals1 = stats[0:8] + beta1 * vals0
    dir_sq1 = norm1 + 2.0 * beta1 * cross1 + beta1 * beta1 * dir_sq0
    res2, step1, stats = advance(res1, grad, vals1, norm1, dir_sq1, beta1)

    coefs = jnp.concatenate([step0, step1, beta1, jnp.zeros((5, LANES), jnp.float32)])
    whole1, whole2 = jnp.concatenate(res1), jnp.concatenate(res2)
    stats, (whole1, whole2, coefs) = small_sum(stats, "param", (whole1, whole2, coefs))
    share = lax.axis_index("walker").astype(jnp.int32).reshape(1)
    base, direction1, res = share_call(share, grad, whole1, whole2, coefs, rows // walkers)
    stats, base, direction1, res = lax.optimization_barrier((stats, base, direction1, res))

    norm2, cross2 = stats[8:9], stats[16:17]
    beta2 = norm2 / norm1
    vals2 = stats[0:8] + beta2 * vals1
    dir_sq2 = norm2 + 2.0 * beta2 * cross2 + beta2 * beta2 * dir_sq1
    squares, _ = small_sum(jnp.sum(vals2 * vals2, axis=0, keepdims=True), "walker")
    step2 = step_length(norm2, squares, rows_all, dir_sq2)
    return (base + step2 * (res + beta2 * direction1)).reshape(-1)


def solution(mesh):
    in_specs = (P("walker", "param"), P("param"))
    out_specs = P(("param", "walker"))
    return jax.shard_map(body, mesh=mesh, in_specs=in_specs, out_specs=out_specs, check_vma=False)
```
